32 devices in a mesh: section: 8 (over y, x, core), tensor: 4 (over z).
Axes of the slice: x: 2, y: 2, z: 4, core: 2. Of those that a mesh axis runs over, the one named last changes fastest.
Arguments:
- inflow: bfloat16 [8, 512, 12288], P('section', 'tensor'), may hold values from -60 to 60
- fresh: bfloat16 [512, 12288], P('tensor'), may hold values from -60 to 60
- stash_held: bfloat16 [8, 512, 12288], P('section', 'tensor'), may hold values from -60 to 60
- grad_in: bfloat16 [8, 512, 12288], P('section', 'tensor'), may hold values from -6 to 6
- query_gain: float32 [8, 12288], P('section', 'tensor'), may hold values from -3 to 3
- key_gain: float32 [8, 12288], P('section', 'tensor'), may hold values from -3 to 3
- value_gain: float32 [8, 12288], P('section', 'tensor'), may hold values from -4 to 4
Outputs:
- first_out: bfloat16 [8, 512, 12288], P('section', 'tensor')
- second_out: bfloat16 [8, 512, 12288], P('section', 'tensor')
- evicted: bfloat16 [8, 512, 12288], P('section', 'tensor')
- grad_out: bfloat16 [8, 512, 12288], P('section', 'tensor')
The draws below stay inside these ranges and needn't reach their ends.
All inputs are finite; a program needn't handle non-finite values.
Results may differ from the reference program's by a relative error of at most 0.0068.
Values may be sent and summed in bfloat16 or wider, within the bound.
A program may use at most 192 MiB of HBM per device.

```python
import jax
import jax.numpy as jnp
from jax import lax

D = 12288
HDIM = 128
SEQ = 512
SECTIONS = 8


def activation(base_key, leading):
    full_shape = leading + (SEQ, D)
    noise_key, row_key, col_key = jax.random.split(base_key, 3)
    noise = jax.random.truncated_normal(noise_key, -4.0, 4.0, full_shape, jnp.float32)
    row_scale = jnp.exp(jax.random.uniform(row_key, leading + (SEQ, 1), jnp.float32, -0.7, 0.7))
    col_scale = jnp.exp(jax.random.uniform(col_key, leading + (1, D), jnp.float32, -0.35, 0.35))
    result = noise * row_scale * col_scale
    return result.astype(jnp.bfloat16)


def gain_draw(base_key):
    return jax.random.truncated_normal(base_key, -3.0, 3.0, (SECTIONS, D), jnp.float32)


def draw_inflow(key, part):
    return activation(jax.random.fold_in(key, 11), (SECTIONS,))


def draw_fresh(key, part):
    return activation(jax.random.fold_in(key, 12), ())


def draw_stash_held(key, part):
    return activation(jax.random.fold_in(key, 13), (SECTIONS,))


def draw_query_gain(key, part):
    return gain_draw(jax.random.fold_in(key, 21))


def draw_key_gain(key, part):
    return gain_draw(jax.random.fold_in(key, 22))


def block_scale(own_key, extent, cuts, low, high):
    gain = 1.0
    for dim, shards_of in cuts:
        steps = jax.random.uniform(jax.random.fold_in(jax.random.fold_in(own_key, 6), dim), (shards_of,), jnp.float32, low / len(cuts), high / len(cuts))
        gain = gain * jnp.repeat(jnp.exp(steps), extent[dim] // shards_of).reshape((-1,) + (1,) * (len(extent) - 1 - dim))
    return gain


def normal_values(key, dims, spread, bound, pieces=(), dtype=jnp.bfloat16):
    drawn = jax.random.normal(key, dims, jnp.float32) * spread
    if len(pieces) > 0:
        drawn = block_scale(key, dims, pieces, -0.22, 0.18) * drawn
    return jnp.clip(drawn, min=-bound, max=bound).astype(dtype)


def setup_inputs(seed: int = 0) -> dict:
    splits = jax.random.split(jax.random.key(seed), 8)
    return {
        "inflow": draw_inflow(jax.random.fold_in(splits[7], 71), 0),
        "fresh": draw_fresh(jax.random.fold_in(splits[7], 71), 0),
        "stash_held": draw_stash_held(jax.random.fold_in(splits[7], 71), 0),
        "grad_in": normal_values(splits[3], (SECTIONS, SEQ, D), 1.0, 6.0, ((0, 8), (1, 4))),
        "query_gain": draw_query_gain(jax.random.fold_in(splits[7], 71), 0),
        "key_gain": draw_key_gain(jax.random.fold_in(splits[7], 71), 0),
        "value_gain": normal_values(splits[6], (SECTIONS, D), 1.0, 4.0, ((0, 8), (1, 4)), jnp.float32),
    }


epsilon = 1e-05
masked_score = -1e+30

def rounded(values):
    return lax.optimization_barrier(values.astype(jnp.bfloat16)).astype(jnp.float32)

def normalize(tokens_in):
    values = tokens_in.astype(jnp.float32)
    factor = lax.rsqrt(lax.optimization_barrier(jnp.mean(values * values, axis=-1, keepdims=True)) + epsilon)
    return (values * factor, factor)

def heads_of(normed, feature_gain):
    scaled = rounded(normed * feature_gain)
    return scaled.reshape(scaled.shape[0], -1, HDIM)

def softmax_causal(queries, key_heads):
    scores = jnp.einsum('ihd,jhd->hij', queries, key_heads) * HDIM ** (-0.5)
    length = queries.shape[0]
    row_index = lax.broadcasted_iota(jnp.int32, (length, length), 0)
    col_index = lax.broadcasted_iota(jnp.int32, (length, length), 1)
    scores = jnp.where(row_index >= col_index, scores, masked_score)
    largest = lax.optimization_barrier(jnp.max(scores, axis=-1, keepdims=True))
    weights = jnp.exp(scores - largest)
    return weights / lax.optimization_barrier(jnp.sum(weights, axis=-1, keepdims=True))

def layer_forward(section_in):
    tokens_in, query_gain, key_gain, value_gain = section_in
    scaled, factor = normalize(tokens_in)
    normed = rounded(scaled)
    queries = heads_of(normed, query_gain)
    key_heads = heads_of(normed, key_gain)
    value_heads = heads_of(normed, value_gain)
    weights = rounded(softmax_causal(queries, key_heads))
    mixed_out = jnp.einsum('hij,jhd->ihd', weights, value_heads)
    mixed_out = rounded(mixed_out.reshape(tokens_in.shape))
    return (tokens_in.astype(jnp.float32) + mixed_out).astype(jnp.bfloat16)

def layer_backward(section_in):
    stash_rows, grad_rows, query_gain, key_gain, value_gain = section_in
    scaled, factor = normalize(stash_rows)
    normed = rounded(scaled)
    queries = heads_of(normed, query_gain)
    key_heads = heads_of(normed, key_gain)
    value_heads = heads_of(normed, value_gain)
    grad_values = grad_rows.astype(jnp.float32)
    cotangent = grad_values.reshape(grad_values.shape[0], -1, HDIM)
    weights = softmax_causal(queries, key_heads)
    weights_low = rounded(weights)
    value_grad = jnp.einsum('hij,ihd->jhd', weights_low, cotangent)
    prob_grad = jnp.einsum('ihd,jhd->hij', cotangent, value_heads)
    score_grad = weights * (prob_grad - lax.optimization_barrier(jnp.sum(prob_grad * weights, axis=-1, keepdims=True)))
    score_low = rounded(score_grad)
    query_grad = jnp.einsum('hij,jhd->ihd', score_low, key_heads) * HDIM ** (-0.5)
    key_grad = jnp.einsum('hij,ihd->jhd', score_low, queries) * HDIM ** (-0.5)
    full_shape = stash_rows.shape
    normed_grad = query_grad.reshape(full_shape) * query_gain + key_grad.reshape(full_shape) * key_gain
    normed_grad = rounded(normed_grad + value_grad.reshape(full_shape) * value_gain)
    inner = lax.optimization_barrier(jnp.mean(normed_grad * scaled, axis=-1, keepdims=True))
    return (grad_values + factor * (normed_grad - scaled * inner)).astype(jnp.bfloat16)

def reference(inflow, fresh, stash_held, grad_in, query_gain, key_gain, value_gain):
    first_out = lax.map(layer_forward, (inflow, query_gain, key_gain, value_gain))
    second_in = jnp.concatenate([fresh[None], first_out[:-1]], axis=0)
    second_out = lax.map(layer_forward, (second_in, query_gain, key_gain, value_gain))
    stash = stash_held[::-1]
    grad_out = lax.map(layer_backward, (stash, grad_in, query_gain, key_gain, value_gain))
    evicted = inflow[::-1]
    return (first_out, second_out, evicted, grad_out)
```

```python
import functools
import math

import jax
import jax.numpy as jnp
from jax import lax
from jax.experimental import pallas as pl
from jax.experimental.pallas import tpu as pltpu
from jax.sharding import PartitionSpec as P

HDIM = 128
ROWS = 128
HEADS_PER_STEP = 2
AXES = ("section", "tensor")

epsilon = 1e-05
masked_score = -1e30
f32 = jnp.float32
bf16 = jnp.bfloat16


def nt(a, b):
    return lax.dot_general(a, b, (((1,), (1,)), ((), ())), preferred_element_type=f32)


def nn(a, b):
    return lax.dot_general(a, b, (((1,), (0,)), ((), ())), preferred_element_type=f32)


def tn(a, b):
    return lax.dot_general(a, b, (((0,), (0,)), ((), ())), preferred_element_type=f32)


def causal(scores, first_row):
    row = lax.broadcasted_iota(jnp.int32, scores.shape, 0) + first_row
    col = lax.broadcasted_iota(jnp.int32, scores.shape, 1)
    return jnp.where(row >= col, scores, masked_score)


def probabilities(scores):
    factor = HDIM ** (-0.5) * math.log2(math.e)
    largest = functools.reduce(
        jnp.maximum, [jnp.max(part, axis=-1, keepdims=True) for part in scores]
    )
    weights = [jnp.exp2((part - largest) * factor) for part in scores]
    total = sum(jnp.sum(part, axis=-1, keepdims=True) for part in weights)
    inverse = 1.0 / total
    return [part * inverse for part in weights]


def projections(x, factor, gains):
    normed = (x.astype(f32) * factor).astype(bf16).astype(f32)
    return [(normed * gain).astype(bf16) for gain in gains]


def forward_kernel(with_low, bias, own, own_r, low, low_r, qg, kg, vg, own_out, *low_out):
    offset = bias[...]
    for head in range(own.shape[1] // HDIM):
        cols = slice(head * HDIM, (head + 1) * HDIM)
        gains = [g[:, cols] for g in (qg, kg, vg)]
        query, key, value = projections(own[:, cols], own_r[...], gains)
        low_query, low_key, low_value = projections(low[:, cols], low_r[...], gains)
        for start in range(0, own.shape[0], ROWS):
            rows = slice(start, start + ROWS)
            seen = slice(0, start + ROWS)
            across = nt(query[rows], low_key) + offset
            within = causal(nt(query[rows], key[seen]), start)
            p_low, p_own = probabilities([across, within])
            mixed = nn(p_low.astype(bf16), low_value) + nn(p_own.astype(bf16), value[seen])
            mixed = mixed.astype(bf16).astype(f32)
            own_out[rows, cols] = (own[rows, cols].astype(f32) + mixed).astype(bf16)
            if with_low:
                within = causal(nt(low_query[rows], low_key[seen]), start)
                (p_own,) = probabilities([within])
                mixed = nn(p_own.astype(bf16), low_value[seen]).astype(bf16).astype(f32)
                low_out[0][rows, cols] = (low[rows, cols].astype(f32) + mixed).astype(bf16)


def backward_kernel(bias, own, own_r, low, low_r, grad, qg, kg, vg, own_out, low_out):
    offset = bias[...]
    scale = HDIM ** (-0.5)
    for head in range(own.shape[1] // HDIM):
        cols = slice(head * HDIM, (head + 1) * HDIM)
        gains = [g[:, cols] for g in (qg, kg, vg)]
        query, key, value = projections(own[:, cols], own_r[...], gains)
        _, low_key, low_value = projections(low[:, cols], low_r[...], gains)
        dlow = jnp.zeros(low_key.shape, f32)
        down = {}
        for start in range(0, own.shape[0], ROWS):
            rows = slice(start, start + ROWS)
            seen = slice(0, start + ROWS)
            g = grad[rows, cols]
            across = nt(query[rows], low_key) + offset
            within = causal(nt(query[rows], key[seen]), start)
            p_low, p_own = probabilities([across, within])
            d_low = nt(g, low_value)
            d_own = nt(g, value[seen])
            inner = jnp.sum(d_low * p_low, axis=-1, keepdims=True) + jnp.sum(
                d_own * p_own, axis=-1, keepdims=True
            )
            s_low = (p_low * (d_low - inner)).astype(bf16)
            s_own = (p_own * (d_own - inner)).astype(bf16)
            dquery = (nn(s_low, low_key) + nn(s_own, key[seen])) * scale
            low_part = tn(s_low, query[rows]) * (scale * gains[1])
            dlow = dlow + low_part + tn(p_low.astype(bf16), g) * gains[2]
            dkey = tn(s_own, query[rows]) * (scale * gains[1])
            dkey = dkey + tn(p_own.astype(bf16), g) * gains[2]
            for at in range(0, start + ROWS, ROWS):
                piece = dkey[at : at + ROWS]
                down[at] = down[at] + piece if at in down else piece
            down[start] = down[start] + dquery * gains[0]
        low_out[:, cols] = dlow.astype(bf16)
        for at, piece in down.items():
            own_out[at : at + ROWS, cols] = piece.astype(bf16)


def call_attention(kernel, outputs, bias, own, own_r, low, low_r, extra, gains):
    half, group = own.shape
    width = HDIM * HEADS_PER_STEP
    if group % width:
        width = HDIM
    wide = pl.BlockSpec((half, width), lambda i: (0, i))
    scalar = pl.BlockSpec((half, 1), lambda i: (0, 0))
    gain = pl.BlockSpec((1, width), lambda i: (0, i))
    return pl.pallas_call(
        kernel,
        grid=(group // width,),
        in_specs=[pl.BlockSpec((1, half), lambda i: (0, 0)), wide, scalar, wide, scalar]
        + [wide] * len(extra)
        + [gain] * 3,
        out_specs=[wide] * outputs,
        out_shape=[jax.ShapeDtypeStruct((half, group), bf16)] * outputs,
        compiler_params=pltpu.CompilerParams(vmem_limit_bytes=32 * 1024 * 1024),
        cost_estimate=pl.CostEstimate(
            flops=half * half * group * 12,
            bytes_accessed=half * group * 8,
            transcendentals=half * half * group // 50,
        ),
    )(bias, own, own_r, low, low_r, *extra, *gains)


def permute(value, route):
    sections, tensors = lax.axis_size("section"), lax.axis_size("tensor")
    pairs = []
    for s in range(sections):
        for z in range(tensors):
            target = route(s, z)
            if target is not None:
                pairs.append((s * tensors + z, target[0] * tensors + target[1]))
    return lax.ppermute(value, AXES, pairs)


def stay(s):
    return s


def first_only(s):
    return s if s == 0 else None


def routes(step, kind, to_section):
    tensors = lax.axis_size("tensor")
    half = tensors // 2

    def route(s, z):
        target = to_section(s)
        if target is None:
            return None
        base = z // half * half
        if kind == "up":
            if base:
                return None
            base = half
        elif kind == "down":
            if not base:
                return None
            base = 0
        return (target, base + (z % half + step) % half)

    return route


def spread(tokens, kind="within", to_section=stay):
    half = lax.axis_size("tensor") // 2
    place = lax.axis_index("tensor") % half
    rows, features = tokens.shape
    group = features // half
    result = jnp.zeros((half * rows, group), tokens.dtype)
    for step in range(half):
        piece = lax.dynamic_slice(tokens, (0, (place + step) % half * group), (rows, group))
        if kind != "within" or step:
            piece = permute(piece, routes(step, kind, to_section))
        result = lax.dynamic_update_slice(result, piece, ((place - step) % half * rows, 0))
    return result


def collect(heads, kind="within"):
    half = lax.axis_size("tensor") // 2
    place = lax.axis_index("tensor") % half
    length, group = heads.shape
    rows = length // half
    result = jnp.zeros((rows, half * group), heads.dtype)
    for step in range(half):
        piece = lax.dynamic_slice(heads, ((place + step) % half * rows, 0), (rows, group))
        if kind != "within" or step:
            piece = permute(piece, routes(step, kind, stay))
        result = lax.dynamic_update_slice(result, piece, (0, (place - step) % half * group))
    return result


def factor_of(tokens):
    values = tokens.astype(f32)
    return lax.rsqrt(jnp.mean(values * values, axis=-1) + epsilon)


def per_device(inflow, fresh, stash_held, grad_in, query_gain, key_gain, value_gain):
    sections, tensors = lax.axis_size("section"), lax.axis_size("tensor")
    section, place = lax.axis_index("section"), lax.axis_index("tensor")
    half = tensors // 2
    upper = place >= half
    inflow, held, grad = inflow[0], stash_held[0], grad_in[0]
    rows, features = inflow.shape
    length = half * rows

    def mirror(s):
        return sections - 1 - s

    inflow_own = spread(inflow)
    inflow_low = spread(inflow, "up")
    stash = permute(held, lambda s, z: (mirror(s), z))
    stash_low = spread(held, "up", mirror)
    grad_own = spread(grad)
    evicted = permute(inflow, lambda s, z: (mirror(s), z))
    fresh_own = spread(fresh, "within", first_only)
    fresh_low = spread(fresh, "up", first_only)

    factors = jnp.stack([factor_of(inflow), factor_of(held), factor_of(fresh)])
    factors = lax.all_gather(factors, "tensor", axis=1, tiled=True)
    stash_factors = permute(factors[1], lambda s, z: (mirror(s), z))

    def halves(values):
        low = values[:length, None]
        own = jnp.where(upper, values[length:, None], low)
        return own, low

    gains = jnp.concatenate([query_gain, key_gain, value_gain], axis=0)
    gains = lax.all_gather(gains, "tensor", axis=1, tiled=True)
    group = features // half
    gains = lax.dynamic_slice(gains, (0, place % half * group), (3, group))
    gains = [gains[i : i + 1] for i in range(3)]
    bias = jnp.where(upper, 0.0, masked_score).astype(f32) * jnp.ones((1, length), f32)

    own_r, low_r = halves(factors[0])
    first_own, first_low = call_attention(
        functools.partial(forward_kernel, True),
        2, bias, inflow_own, own_r, inflow_low, low_r, [], gains,
    )

    def onward(s, z):
        return (s + 1, z) if s + 1 < sections else None

    def onward_upper(s, z):
        return onward(s, z) if z >= half else None

    def squares(values):
        values = values.astype(f32)
        return jnp.sum(values * values, axis=-1)

    moved_own = permute(first_own, onward)
    moved_low = permute(first_low, onward_upper)
    sums = jnp.stack([squares(first_own), squares(first_low)])
    sums = lax.all_gather(sums, "tensor")
    sums = jnp.sum(lax.dynamic_slice_in_dim(sums, place // half * half, half, 0), axis=0)
    second_factors = permute(lax.rsqrt(sums / features + epsilon), onward)
    first_out = collect(first_own)

    stash_own = spread(stash)
    own_r, low_r = halves(stash_factors)
    dnormed_own, dnormed_low = call_attention(
        backward_kernel, 2, bias, stash_own, own_r, stash_low, low_r, [grad_own], gains
    )
    returned_low = collect(dnormed_low, "down")
    returned_own = collect(dnormed_own)

    is_first = section == 0
    own_r, low_r = halves(factors[2])
    second_own = jnp.where(is_first, fresh_own, moved_own)
    second_low = jnp.where(is_first, fresh_low, moved_low)
    own_r = jnp.where(is_first, own_r, second_factors[0][:, None])
    low_r = jnp.where(is_first, low_r, second_factors[1][:, None])
    (second_heads,) = call_attention(
        functools.partial(forward_kernel, False),
        1, bias, second_own, own_r, second_low, low_r, [], gains,
    )
    second_out = collect(second_heads)

    returned = returned_own.astype(f32) + returned_low.astype(f32)
    factor = factor_of(stash)[:, None]
    scaled = stash.astype(f32) * factor
    inner = jnp.mean(returned * scaled, axis=-1, keepdims=True)
    grad_out = (grad.astype(f32) + factor * (returned - scaled * inner)).astype(bf16)
    return (first_out[None], second_out[None], evicted[None], grad_out[None])


def solution(mesh):
    tokens = P("section", "tensor", None)
    gain = P("section", "tensor")
    return jax.shard_map(
        per_device,
        mesh=mesh,
        in_specs=(tokens, P("tensor", None), tokens, tokens, gain, gain, gain),
        out_specs=(tokens,) * 4,
        check_vma=False,
    )
```

```python
import functools
import math

import jax
import jax.numpy as jnp
from jax import lax
from jax.experimental import pallas as pl
from jax.experimental.pallas import tpu as pltpu
from jax.sharding import PartitionSpec as P

HDIM = 128
ROWS = 128
LANES = 128
CHUNKS = 2
MESH = pl.DeviceIdType.MESH

epsilon = 1e-05
masked_score = -1e30
f32 = jnp.float32
bf16 = jnp.bfloat16


def nt(a, b):
    return lax.dot_general(a, b, (((1,), (1,)), ((), ())), preferred_element_type=f32)


def nn(a, b):
    return lax.dot_general(a, b, (((1,), (0,)), ((), ())), preferred_element_type=f32)


def projections(x, factor, gains):
    normed = (x.astype(f32) * factor).astype(bf16).astype(f32)
    return [(normed * gain).astype(bf16) for gain in gains]


def exponentials(keys, queries):
    factor = HDIM ** (-0.5) * math.log2(math.e)
    scores = nt(keys, queries)
    count = queries.shape[0]
    before = scores.shape[0] - count
    row = lax.broadcasted_iota(jnp.int32, (count, count), 1)
    col = lax.broadcasted_iota(jnp.int32, (count, count), 0)
    last = jnp.where(row >= col, scores[before:], masked_score)
    if before:
        scores = jnp.concatenate([scores[:before], last], axis=0)
    else:
        scores = last
    largest = jnp.max(scores, axis=0, keepdims=True)
    weights = jnp.exp2((scores - largest) * factor)
    return weights, 1.0 / jnp.sum(weights, axis=0, keepdims=True)


def attend(x, out, sums, cols, query, key, value, base):
    turned = value.T
    for start in range(0, query.shape[0], ROWS):
        rows = slice(start, start + ROWS)
        seen = base + start + ROWS
        weights, inverse = exponentials(key[:seen], query[rows])
        mixed = (nn(turned[:, :seen], weights.astype(bf16)) * inverse).T
        mixed = mixed.astype(bf16).astype(f32)
        result = (x[rows, cols].astype(f32) + mixed).astype(bf16)
        out[rows, cols] = result
        if sums is not None:
            result = result.astype(f32)
            sums[rows, :] += result * result


def derive(grad, cols, query, key, value, base, gains):
    scale = HDIM ** (-0.5)
    turned = key.T
    total = {}
    for start in range(0, query.shape[0], ROWS):
        rows = slice(start, start + ROWS)
        seen = base + start + ROWS
        g = grad[rows, cols]
        weights, inverse = exponentials(key[:seen], query[rows])
        weights = weights * inverse
        dprob = nt(value[:seen], g)
        inner = jnp.sum(dprob * weights, axis=0, keepdims=True)
        dscore = (weights * (dprob - inner)).astype(bf16)
        dquery = nn(turned[:, :seen], dscore).T * (scale * gains[0])
        part = nn(dscore, query[rows]) * (scale * gains[1])
        part = part + nn(weights.astype(bf16), g) * gains[2]
        for at in range(0, seen, ROWS):
            piece = part[at : at + ROWS]
            if at == seen - ROWS:
                piece = piece + dquery
            total[at] = total[at] + piece if at in total else piece
    return total


def each_head(begin, width, body):
    count = width // HDIM
    together = 2 if count % 2 == 0 else 1

    def step(index, carry):
        for offset in range(together):
            at = begin + (index * together + offset) * HDIM
            body(pl.ds(pl.multiple_of(at, HDIM), HDIM))
        return carry

    lax.fori_loop(0, count // together, step, 0)


def kernel(
    sections, tensors,
    inflow, fresh, held, grad, inflow_sums, fresh_sums, held_sums, gains_in,
    first_out, second_out, evicted, stash, returned_own, returned_low,
    x_own, x_low, st_own, st_low, g_own, m_own, m_low, f_own, f_low, dn_own, dn_low, s_own,
    xs_own, xs_low, ss_own, ss_low, ms_own, ms_low, fs_own, fs_low, gains,
    send_sems, recv_sems, local_sems,
):
    half = tensors // 2
    rows, features = inflow.shape
    length = half * rows
    group = features // half
    part = group // CHUNKS
    section, place = lax.axis_index("section"), lax.axis_index("tensor")
    mirror = sections - 1 - section
    inner = lax.rem(place, half)
    base = place - inner
    upper = place >= half
    lower = place < half
    is_first = section == 0
    has_next = section + 1 < sections
    has_before = section > 0
    always = None
    counters = {"remote": 0, "local": 0}
    pending = []

    def guarded(condition, action):
        if condition is always:
            action()
        else:
            pl.when(condition)(action)

    def both(a, b):
        return a if b is always else b if a is always else jnp.logical_and(a, b)

    class Copy:
        def __init__(self, source, there, landing, target, sends=always, gets=always):
            index = counters["remote"]
            counters["remote"] += 1
            self.sends, self.gets = sends, gets
            self.out = pltpu.make_async_remote_copy(
                src_ref=source, dst_ref=there, send_sem=send_sems.at[index],
                recv_sem=recv_sems.at[index], device_id=target, device_id_type=MESH,
            )
            self.into = pltpu.make_async_remote_copy(
                src_ref=landing, dst_ref=landing, send_sem=send_sems.at[index],
                recv_sem=recv_sems.at[index], device_id=target, device_id_type=MESH,
            )
            pending.append(self)

        def start(self):
            guarded(self.sends, self.out.start)

        def receive(self):
            guarded(self.gets, self.into.wait_recv)

        def sent(self):
            if self in pending:
                pending.remove(self)
                guarded(self.sends, self.out.wait_send)

    class Local:
        def __init__(self, source, target, condition=always):
            index = counters["local"]
            counters["local"] += 1
            self.condition = condition
            self.copy = pltpu.make_async_copy(source, target, local_sems.at[index])

        def start(self):
            guarded(self.condition, self.copy.start)

        def receive(self):
            guarded(self.condition, self.copy.wait)

        def sent(self):
            pass

    def turn(step):
        return lax.rem(inner + step, half), lax.rem(inner + half - step, half)

    def columns(which, chunk):
        return pl.ds(pl.multiple_of(which * group + chunk * part, LANES), part)

    def block(which):
        return pl.ds(pl.multiple_of(which * rows, 16), rows)

    def to_heads(tokens, heads, chunk, kind, to_section, condition=always):
        copies = []
        own_cols = pl.ds(chunk * part, part)
        for step in range(half):
            ahead, behind = turn(step)
            source = tokens.at[:, columns(ahead, chunk)]
            there = heads.at[block(inner), own_cols]
            landing = heads.at[block(behind), own_cols]
            if kind == "up":
                copies.append(Copy(
                    source, there, landing, (to_section, half + ahead),
                    both(lower, condition), both(upper, condition),
                ))
            elif step == 0:
                copies.append(Local(source, there, condition))
            else:
                copies.append(Copy(source, there, landing, (to_section, base + ahead), condition, condition))
        return copies

    def to_tokens(heads, tokens, chunk, kind):
        copies = []
        own_cols = pl.ds(chunk * part, part)
        for step in range(half):
            ahead, behind = turn(step)
            source = heads.at[block(ahead), own_cols]
            there = tokens.at[:, columns(inner, chunk)]
            landing = tokens.at[:, columns(behind, chunk)]
            if kind == "down":
                copies.append(Copy(source, there, landing, (section, ahead), upper, lower))
            elif step == 0:
                copies.append(Local(source, there))
            else:
                copies.append(Copy(source, there, landing, (section, base + ahead)))
        return copies

    def sums_to(source, target, kind, to_section, condition=always):
        copies = []
        for step in range(half):
            ahead, behind = turn(step)
            there, landing = target(inner), target(behind)
            if kind == "up":
                copies.append(Copy(
                    source, there, landing, (to_section, half + ahead),
                    both(lower, condition), both(upper, condition),
                ))
            elif step == 0 and kind == "within":
                copies.append(Local(source, there, condition))
            else:
                copies.append(Copy(source, there, landing, (to_section, base + ahead), condition, condition))
        return copies

    def run(copies):
        for copy in copies:
            copy.start()
        return copies

    def arrive(*lists):
        for copies in lists:
            for copy in copies:
                copy.receive()

    def left(copies):
        for copy in copies:
            copy.sent()

    barrier = pltpu.get_barrier_semaphore()

    def greet(to_section, to_place):
        pl.semaphore_signal(barrier, inc=1, device_id=(to_section, to_place), device_id_type=MESH)

    for step in range(1, tensors):
        greet(section, lax.rem(place + step, tensors))
    for step in range(tensors):
        greet(mirror, lax.rem(place + step, tensors))

    @pl.when(has_next)
    def _():
        for step in range(half):
            greet(section + 1, base + turn(step)[0])

    @pl.when(has_before)
    def _():
        for step in range(half):
            greet(section - 1, base + turn(step)[0])

    neighbours = has_next.astype(jnp.int32) + has_before.astype(jnp.int32)
    pl.semaphore_wait(barrier, 2 * tensors - 1 + half * neighbours)

    share = features // tensors
    pair = place // 2
    gain_copies = []
    for parity in range(2):
        there = gains.at[:, pl.ds(parity * share, share)]
        mine = lax.rem(place, 2) == parity
        for to in (0, half):
            target = to + pair
            self_copy = both(mine, target == place)
            from_me = 2 * inner + parity == place
            in_half = base == to
            gain_copies.append(Copy(
                gains_in, there, there, (section, target),
                both(mine, target != place), both(in_half, jnp.logical_not(from_me)),
            ))
            gain_copies.append(Local(gains_in, there, self_copy))
    run(gain_copies)

    def rows_of(ref):
        return lambda which: ref.at[block(which)]

    def slots_of(ref):
        return lambda which: ref.at[:, block(which)]

    inflow_factors = run(
        sums_to(inflow_sums, rows_of(xs_low), "up", section) + sums_to(inflow_sums, rows_of(xs_own), "within", section)
    )
    up_inflow = [to_heads(inflow, x_low, chunk, "up", section) for chunk in range(CHUNKS)]
    own_inflow = [to_heads(inflow, x_own, chunk, "within", section) for chunk in range(CHUNKS)]
    run(up_inflow[0] + own_inflow[0])
    mirror_stash = run([Copy(held, stash, stash, (mirror, place))])
    run(up_inflow[1] + own_inflow[1])
    stash_factors = run(
        sums_to(held_sums, rows_of(ss_low), "up", mirror) + sums_to(held_sums, rows_of(ss_own), "away", mirror)
    )
    own_grad = [to_heads(grad, g_own, chunk, "within", section) for chunk in range(CHUNKS)]
    up_stash = [to_heads(held, st_low, chunk, "up", mirror) for chunk in range(CHUNKS)]
    own_stash = [to_heads(stash, st_own, chunk, "within", section) for chunk in range(CHUNKS)]
    up_fresh = [to_heads(fresh, m_low, chunk, "up", section, is_first) for chunk in range(CHUNKS)]
    own_fresh = [to_heads(fresh, m_own, chunk, "within", section, is_first) for chunk in range(CHUNKS)]
    fresh_factors = sums_to(fresh_sums, slots_of(ms_low), "up", section, is_first) + sums_to(
        fresh_sums, slots_of(ms_own), "within", section, is_first
    )
    mirror_inflow = [Copy(inflow, evicted, evicted, (mirror, place))]

    fs_own[...] = jnp.zeros_like(fs_own)
    fs_low[...] = jnp.zeros_like(fs_low)

    def factor(total):
        return lax.rsqrt(jnp.sum(total, axis=-1, keepdims=True) / features + epsilon)

    def gains_of(cols):
        return [gains[i : i + 1, cols] for i in range(3)]

    def forward(chunk, own, low, own_total, low_total, own_out, low_out, own_sums, low_sums):
        @pl.when(upper)
        def _():
            own_factor, low_factor = factor(own_total()), factor(low_total())

            def head(cols):
                g = gains_of(cols)
                query, key, value = projections(own[:, cols], own_factor, g)
                low_query, low_key, low_value = projections(low[:, cols], low_factor, g)
                keys = jnp.concatenate([low_key, key], axis=0)
                values = jnp.concatenate([low_value, value], axis=0)
                attend(own, own_out, own_sums, cols, query, keys, values, length)
                if low_out is not None:
                    attend(low, low_out, low_sums, cols, low_query, low_key, low_value, 0)

            each_head(chunk * part, part, head)

        @pl.when(lower)
        def _():
            own_factor = factor(own_total())

            def head(cols):
                query, key, value = projections(own[:, cols], own_factor, gains_of(cols))
                attend(own, own_out, own_sums, cols, query, key, value, 0)

            each_head(chunk * part, part, head)

    def backward(chunk):
        @pl.when(upper)
        def _():
            own_factor, low_factor = factor(ss_own[...]), factor(ss_low[...])

            def head(cols):
                g = gains_of(cols)
                query, key, value = projections(st_own[:, cols], own_factor, g)
                low_key, low_value = projections(st_low[:, cols], low_factor, g[1:])
                keys = jnp.concatenate([low_key, key], axis=0)
                values = jnp.concatenate([low_value, value], axis=0)
                for at, piece in derive(g_own, cols, query, keys, values, length, g).items():
                    if at < length:
                        dn_low[at : at + ROWS, cols] = piece.astype(bf16)
                    else:
                        dn_own[at - length : at - length + ROWS, cols] = piece.astype(bf16)

            each_head(chunk * part, part, head)

        @pl.when(lower)
        def _():
            own_factor = factor(ss_own[...])

            def head(cols):
                g = gains_of(cols)
                query, key, value = projections(st_own[:, cols], own_factor, g)
                for at, piece in derive(g_own, cols, query, key, value, 0, g).items():
                    dn_own[at : at + ROWS, cols] = piece.astype(bf16)

            each_head(chunk * part, part, head)

    next_upper = both(has_next, upper)
    before_upper = both(has_before, upper)
    relays, firsts = [], []
    for chunk in range(CHUNKS):
        if chunk == 0:
            arrive(gain_copies, inflow_factors)
        arrive(up_inflow[chunk], own_inflow[chunk])
        forward(
            chunk, x_own, x_low, lambda: xs_own[...], lambda: xs_low[...],
            f_own, f_low, fs_own, fs_low,
        )
        cols = pl.ds(chunk * part, part)
        relays += run([
            Copy(f_own.at[:, cols], m_own.at[:, cols], m_own.at[:, cols], (section + 1, place), has_next, has_before),
            Copy(f_low.at[:, cols], m_low.at[:, cols], m_low.at[:, cols], (section + 1, place), next_upper, before_upper),
        ])
        left(up_inflow[chunk])
        run(up_stash[chunk])
        if chunk == 0:
            arrive(mirror_stash)
        run(own_grad[chunk] + own_stash[chunk])
        firsts += run(to_tokens(f_own, first_out, chunk, "within"))

    for step in range(half):
        ahead, behind = turn(step)
        relays += run([
            Copy(fs_own, ms_own.at[inner], ms_own.at[behind], (section + 1, base + ahead), has_next, has_before),
            Copy(fs_low, ms_low.at[inner], ms_low.at[behind], (section + 1, base + ahead), next_upper, before_upper),
        ])
    run(mirror_inflow)

    backs = []
    for chunk in range(CHUNKS):
        if chunk == 0:
            arrive(stash_factors)
        arrive(up_stash[chunk], own_grad[chunk], own_stash[chunk])
        left(up_stash[chunk])
        run(up_fresh[chunk] + own_fresh[chunk])
        if chunk == 0:
            run(fresh_factors)
        backward(chunk)
        backs += run(to_tokens(dn_low, returned_low, chunk, "down") + to_tokens(dn_own, returned_own, chunk, "within"))

    arrive(relays, fresh_factors, *up_fresh, *own_fresh)
    seconds = []
    for chunk in range(CHUNKS):
        forward(
            chunk, m_own, m_low, lambda: jnp.sum(ms_own[...], axis=0), lambda: jnp.sum(ms_low[...], axis=0),
            s_own, None, None, None,
        )
        seconds += run(to_tokens(s_own, second_out, chunk, "within"))
    arrive(firsts, mirror_inflow, backs, seconds)
    for copy in list(pending):
        copy.sent()


def counts(half):
    remote = CHUNKS * (9 * half + 2) + 9 * half + 16
    return remote, CHUNKS * 8 + 16


def row_sums(tokens):
    values = tokens.astype(f32)
    return jnp.pad(jnp.sum(values * values, axis=-1, keepdims=True), ((0, 0), (0, LANES - 1)))


def per_device(inflow, fresh, stash_held, grad_in, query_gain, key_gain, value_gain):
    sections, tensors = lax.axis_size("section"), lax.axis_size("tensor")
    half = tensors // 2
    inflow, held, grad = inflow[0], stash_held[0], grad_in[0]
    rows, features = inflow.shape
    length, group = half * rows, features // half
    gains_in = jnp.pad(
        jnp.concatenate([query_gain, key_gain, value_gain], axis=0), ((0, 5), (0, 0))
    )
    fresh_sums = jnp.pad(row_sums(fresh)[None], ((0, half - 1), (0, 0), (0, 0)))
    tokens = jax.ShapeDtypeStruct((rows, features), bf16)
    any_space = pl.BlockSpec(memory_space=pl.ANY)
    wide = pltpu.VMEM((length, group), bf16)
    narrow = pltpu.VMEM((length, LANES), f32)
    slots = pltpu.VMEM((half, length, LANES), f32)
    remote, local = counts(half)
    first_out, second_out, evicted, stash, returned_own, returned_low = pl.pallas_call(
        functools.partial(kernel, sections, tensors),
        in_specs=[any_space] * 8,
        out_specs=[any_space] * 6,
        out_shape=[tokens] * 6,
        scratch_shapes=[wide] * 12
        + [narrow] * 4
        + [slots] * 2
        + [narrow] * 2
        + [pltpu.VMEM((8, group), f32)]
        + [
            pltpu.SemaphoreType.DMA((remote,)),
            pltpu.SemaphoreType.DMA((remote,)),
            pltpu.SemaphoreType.DMA((local,)),
        ],
        compiler_params=pltpu.CompilerParams(
            collective_id=0, has_side_effects=True, vmem_limit_bytes=54 * 1024 * 1024
        ),
        cost_estimate=pl.CostEstimate(
            flops=length * length * group * 40,
            bytes_accessed=length * group * 40,
            transcendentals=length * length * group // 16,
        ),
    )(inflow, fresh, held, grad, row_sums(inflow), fresh_sums, row_sums(held), gains_in)

    received = lax.axis_index("tensor") < half
    returned = returned_own.astype(f32) + jnp.where(received, returned_low.astype(f32), 0.0)
    values = stash.astype(f32)
    factor = lax.rsqrt(jnp.mean(values * values, axis=-1, keepdims=True) + epsilon)
    scaled = values * factor
    inner = jnp.mean(returned * scaled, axis=-1, keepdims=True)
    grad_out = (grad.astype(f32) + factor * (returned - scaled * inner)).astype(bf16)
    return (first_out[None], second_out[None], evicted[None], grad_out[None])


def solution(mesh):
    tokens = P("section", "tensor", None)
    gain = P("section", "tensor")
    return jax.shard_map(
        per_device,
        mesh=mesh,
        in_specs=(tokens, P("tensor", None), tokens, tokens, gain, gain, gain),
        out_specs=(tokens,) * 4,
        check_vma=False,
    )
```

```python
import functools
import math

import jax
import jax.numpy as jnp
from jax import lax
from jax.experimental import pallas as pl
from jax.experimental.pallas import tpu as pltpu
from jax.sharding import PartitionSpec as P

HDIM = 128
ROWS = 128
LANES = 128
CHUNKS = 3
MESH = pl.DeviceIdType.MESH

epsilon = 1e-05
masked_score = -1e30
f32 = jnp.float32
bf16 = jnp.bfloat16


def nt(a, b):
    return lax.dot_general(a, b, (((1,), (1,)), ((), ())), preferred_element_type=f32)


def nn(a, b):
    return lax.dot_general(a, b, (((1,), (0,)), ((), ())), preferred_element_type=f32)


def projections(x, factor, gains):
    normed = (x.astype(f32) * factor).astype(bf16).astype(f32)
    return [(normed * gain).astype(bf16) for gain in gains]


def exponentials(keys, queries):
    factor = HDIM ** (-0.5) * math.log2(math.e)
    scores = nt(keys, queries)
    count = queries.shape[0]
    before = scores.shape[0] - count
    row = lax.broadcasted_iota(jnp.int32, (count, count), 1)
    col = lax.broadcasted_iota(jnp.int32, (count, count), 0)
    last = jnp.where(row >= col, scores[before:], masked_score)
    if before:
        scores = jnp.concatenate([scores[:before], last], axis=0)
    else:
        scores = last
    largest = jnp.max(scores, axis=0, keepdims=True)
    weights = jnp.exp2((scores - largest) * factor)
    return weights, 1.0 / jnp.sum(weights, axis=0, keepdims=True)


def attend(x, out, sums, cols, query, key, value, base):
    turned = value.T
    for start in range(0, query.shape[0], ROWS):
        rows = slice(start, start + ROWS)
        seen = base + start + ROWS
        weights, inverse = exponentials(key[:seen], query[rows])
        mixed = (nn(turned[:, :seen], weights.astype(bf16)) * inverse).T
        mixed = mixed.astype(bf16).astype(f32)
        result = (x[rows, cols].astype(f32) + mixed).astype(bf16)
        out[rows, cols] = result
        if sums is not None:
            result = result.astype(f32)
            sums[rows, :] += result * result


def derive(grad, cols, query, key, value, base, gains):
    scale = HDIM ** (-0.5)
    turned = key.T
    total = {}
    for start in range(0, query.shape[0], ROWS):
        rows = slice(start, start + ROWS)
        seen = base + start + ROWS
        g = grad[rows, cols]
        weights, inverse = exponentials(key[:seen], query[rows])
        weights = weights * inverse
        dprob = nt(value[:seen], g)
        inner = jnp.sum(dprob * weights, axis=0, keepdims=True)
        dscore = (weights * (dprob - inner)).astype(bf16)
        dquery = nn(turned[:, :seen], dscore).T * (scale * gains[0])
        part = nn(dscore, query[rows]) * (scale * gains[1])
        part = part + nn(weights.astype(bf16), g) * gains[2]
        for at in range(0, seen, ROWS):
            piece = part[at : at + ROWS]
            if at == seen - ROWS:
                piece = piece + dquery
            total[at] = total[at] + piece if at in total else piece
    return total


def each_head(begin, width, body):
    count = width // HDIM
    together = 2 if count % 2 == 0 else 1

    def step(index, carry):
        for offset in range(together):
            at = begin + (index * together + offset) * HDIM
            body(pl.ds(pl.multiple_of(at, HDIM), HDIM))
        return carry

    lax.fori_loop(0, count // together, step, 0)


def kernel(
    sections, tensors,
    inflow, fresh, held, grad, gains_in,
    first_out, second_out, evicted, stash, returned_own, returned_low,
    x_own, x_low, st_own, st_low, g_own, m_own, m_low, f_own, f_low, dn_own, dn_low, s_own,
    xs_own, xs_low, ss_own, ss_low, ms_own, ms_low, fs_own, fs_low, gains,
    inflow_here, held_here, fresh_here, inflow_sums, held_sums, fresh_sums,
    send_sems, recv_sems, local_sems,
):
    half = tensors // 2
    rows, features = inflow.shape
    length = half * rows
    group = features // half
    part = group // CHUNKS
    section, place = lax.axis_index("section"), lax.axis_index("tensor")
    mirror = sections - 1 - section
    inner = lax.rem(place, half)
    base = place - inner
    upper = place >= half
    lower = place < half
    is_first = section == 0
    has_next = section + 1 < sections
    has_before = section > 0
    always = None
    counters = {"remote": 0, "local": 0}
    pending = []

    def guarded(condition, action):
        if condition is always:
            action()
        else:
            pl.when(condition)(action)

    def both(a, b):
        return a if b is always else b if a is always else jnp.logical_and(a, b)

    class Copy:
        def __init__(self, source, there, landing, target, sends=always, gets=always):
            index = counters["remote"]
            counters["remote"] += 1
            self.sends, self.gets = sends, gets
            self.out = pltpu.make_async_remote_copy(
                src_ref=source, dst_ref=there, send_sem=send_sems.at[index],
                recv_sem=recv_sems.at[index], device_id=target, device_id_type=MESH,
            )
            self.into = pltpu.make_async_remote_copy(
                src_ref=landing, dst_ref=landing, send_sem=send_sems.at[index],
                recv_sem=recv_sems.at[index], device_id=target, device_id_type=MESH,
            )
            pending.append(self)

        def start(self):
            guarded(self.sends, self.out.start)

        def receive(self):
            guarded(self.gets, self.into.wait_recv)

        def sent(self):
            if self in pending:
                pending.remove(self)
                guarded(self.sends, self.out.wait_send)

    class Local:
        def __init__(self, source, target, condition=always):
            index = counters["local"]
            counters["local"] += 1
            self.condition = condition
            self.copy = pltpu.make_async_copy(source, target, local_sems.at[index])

        def start(self):
            guarded(self.condition, self.copy.start)

        def receive(self):
            guarded(self.condition, self.copy.wait)

        def sent(self):
            pass

    def turn(step):
        return lax.rem(inner + step, half), lax.rem(inner + half - step, half)

    def columns(which, chunk):
        return pl.ds(pl.multiple_of(which * group + chunk * part, LANES), part)

    def block(which):
        return pl.ds(pl.multiple_of(which * rows, 16), rows)

    def to_heads(tokens, heads, chunk, kind, to_section, condition=always):
        copies = []
        own_cols = pl.ds(chunk * part, part)
        for step in range(half):
            ahead, behind = turn(step)
            source = tokens.at[:, columns(ahead, chunk)]
            there = heads.at[block(inner), own_cols]
            landing = heads.at[block(behind), own_cols]
            if kind == "up":
                copies.append(Copy(
                    source, there, landing, (to_section, half + ahead),
                    both(lower, condition), both(upper, condition),
                ))
            elif step == 0:
                copies.append(Local(source, there, condition))
            else:
                copies.append(Copy(source, there, landing, (to_section, base + ahead), condition, condition))
        return copies

    def to_tokens(heads, tokens, chunk, kind):
        copies = []
        own_cols = pl.ds(chunk * part, part)
        for step in range(half):
            ahead, behind = turn(step)
            source = heads.at[block(ahead), own_cols]
            there = tokens.at[:, columns(inner, chunk)]
            landing = tokens.at[:, columns(behind, chunk)]
            if kind == "down":
                copies.append(Copy(source, there, landing, (section, ahead), upper, lower))
            elif step == 0:
                copies.append(Local(source, there))
            else:
                copies.append(Copy(source, there, landing, (section, base + ahead)))
        return copies

    def sums_to(source, target, kind, to_section, condition=always):
        copies = []
        for step in range(half):
            ahead, behind = turn(step)
            there, landing = target(inner), target(behind)
            if kind == "up":
                copies.append(Copy(
                    source, there, landing, (to_section, half + ahead),
                    both(lower, condition), both(upper, condition),
                ))
            elif step == 0 and kind == "within":
                copies.append(Local(source, there, condition))
            else:
                copies.append(Copy(source, there, landing, (to_section, base + ahead), condition, condition))
        return copies

    def run(copies):
        for copy in copies:
            copy.start()
        return copies

    def arrive(*lists):
        for copies in lists:
            for copy in copies:
                copy.receive()

    def left(copies):
        for copy in copies:
            copy.sent()

    barrier = pltpu.get_barrier_semaphore()

    def greet(to_section, to_place):
        pl.semaphore_signal(barrier, inc=1, device_id=(to_section, to_place), device_id_type=MESH)

    for step in range(1, tensors):
        greet(section, lax.rem(place + step, tensors))
    for step in range(tensors):
        greet(mirror, lax.rem(place + step, tensors))

    @pl.when(has_next)
    def _():
        for step in range(half):
            greet(section + 1, base + turn(step)[0])

    @pl.when(has_before)
    def _():
        for step in range(half):
            greet(section - 1, base + turn(step)[0])

    neighbours = has_next.astype(jnp.int32) + has_before.astype(jnp.int32)
    pl.semaphore_wait(barrier, 2 * tensors - 1 + half * neighbours)

    share = features // tensors
    pair = place // 2
    gain_copies = []
    for parity in range(2):
        there = gains.at[:, pl.ds(parity * share, share)]
        mine = lax.rem(place, 2) == parity
        for to in (0, half):
            target = to + pair
            self_copy = both(mine, target == place)
            from_me = 2 * inner + parity == place
            in_half = base == to
            gain_copies.append(Copy(
                gains_in, there, there, (section, target),
                both(mine, target != place), both(in_half, jnp.logical_not(from_me)),
            ))
            gain_copies.append(Local(gains_in, there, self_copy))
    run(gain_copies)

    def rows_of(ref):
        return lambda which: ref.at[block(which)]

    def slots_of(ref):
        return lambda which: ref.at[:, block(which)]

    loads = run([Local(inflow, inflow_here), Local(held, held_here), Local(fresh, fresh_here)])
    inflow_factors = sums_to(inflow_sums, rows_of(xs_low), "up", section) + sums_to(
        inflow_sums, rows_of(xs_own), "within", section
    )
    up_inflow = [to_heads(inflow, x_low, chunk, "up", section) for chunk in range(CHUNKS)]
    own_inflow = [to_heads(inflow, x_own, chunk, "within", section) for chunk in range(CHUNKS)]
    run(up_inflow[0] + own_inflow[0])
    mirror_stash = run([Copy(held, stash, stash, (mirror, place))])
    stash_factors = sums_to(held_sums, rows_of(ss_low), "up", mirror) + sums_to(
        held_sums, rows_of(ss_own), "away", mirror
    )
    own_grad = [to_heads(grad, g_own, chunk, "within", section) for chunk in range(CHUNKS)]
    up_stash = [to_heads(stash, st_low, chunk, "up", section) for chunk in range(CHUNKS)]
    own_stash = [to_heads(stash, st_own, chunk, "within", section) for chunk in range(CHUNKS)]
    up_fresh = [to_heads(fresh, m_low, chunk, "up", section, is_first) for chunk in range(CHUNKS)]
    own_fresh = [to_heads(fresh, m_own, chunk, "within", section, is_first) for chunk in range(CHUNKS)]
    fresh_factors = sums_to(fresh_sums, slots_of(ms_low), "up", section, is_first) + sums_to(
        fresh_sums, slots_of(ms_own), "within", section, is_first
    )
    mirror_inflow = [Copy(inflow, evicted, evicted, (mirror, place))]

    def add_squares(tokens, sums):
        sums[...] = jnp.zeros_like(sums)

        def tile(cols):
            values = tokens[:, cols].astype(f32)
            sums[...] += values * values

        each_head(0, features, tile)

    arrive(loads)
    add_squares(inflow_here, inflow_sums)
    run(inflow_factors)
    for chunk in range(1, CHUNKS):
        run(up_inflow[chunk] + own_inflow[chunk])
    add_squares(held_here, held_sums)
    run(stash_factors)
    for chunk in range(CHUNKS):
        run(own_grad[chunk])
    fresh_sums[...] = jnp.zeros_like(fresh_sums)
    add_squares(fresh_here, fresh_sums.at[0])
    fs_own[...] = jnp.zeros_like(fs_own)
    fs_low[...] = jnp.zeros_like(fs_low)

    def factor(total):
        return lax.rsqrt(jnp.sum(total, axis=-1, keepdims=True) / features + epsilon)

    def gains_of(cols):
        return [gains[i : i + 1, cols] for i in range(3)]

    def forward(chunk, own, low, own_total, low_total, own_out, low_out, own_sums, low_sums):
        @pl.when(upper)
        def _():
            own_factor, low_factor = factor(own_total()), factor(low_total())

            def head(cols):
                g = gains_of(cols)
                query, key, value = projections(own[:, cols], own_factor, g)
                low_query, low_key, low_value = projections(low[:, cols], low_factor, g)
                keys = jnp.concatenate([low_key, key], axis=0)
                values = jnp.concatenate([low_value, value], axis=0)
                attend(own, own_out, own_sums, cols, query, keys, values, length)
                if low_out is not None:
                    attend(low, low_out, low_sums, cols, low_query, low_key, low_value, 0)

            each_head(chunk * part, part, head)

        @pl.when(lower)
        def _():
            own_factor = factor(own_total())

            def head(cols):
                query, key, value = projections(own[:, cols], own_factor, gains_of(cols))
                attend(own, own_out, own_sums, cols, query, key, value, 0)

            each_head(chunk * part, part, head)

    def backward(chunk):
        @pl.when(upper)
        def _():
            own_factor, low_factor = factor(ss_own[...]), factor(ss_low[...])

            def head(cols):
                g = gains_of(cols)
                query, key, value = projections(st_own[:, cols], own_factor, g)
                low_key, low_value = projections(st_low[:, cols], low_factor, g[1:])
                keys = jnp.concatenate([low_key, key], axis=0)
                values = jnp.concatenate([low_value, value], axis=0)
                for at, piece in derive(g_own, cols, query, keys, values, length, g).items():
                    if at < length:
                        dn_low[at : at + ROWS, cols] = piece.astype(bf16)
                    else:
                        dn_own[at - length : at - length + ROWS, cols] = piece.astype(bf16)

            each_head(chunk * part, part, head)

        @pl.when(lower)
        def _():
            own_factor = factor(ss_own[...])

            def head(cols):
                g = gains_of(cols)
                query, key, value = projections(st_own[:, cols], own_factor, g)
                for at, piece in derive(g_own, cols, query, key, value, 0, g).items():
                    dn_own[at : at + ROWS, cols] = piece.astype(bf16)

            each_head(chunk * part, part, head)

    next_upper = both(has_next, upper)
    before_upper = both(has_before, upper)
    relays, firsts = [], []
    for chunk in range(CHUNKS):
        if chunk == 0:
            arrive(gain_copies, inflow_factors)
        arrive(up_inflow[chunk], own_inflow[chunk])
        if chunk == 0:
            arrive(mirror_stash)
        left(up_inflow[chunk])
        run(up_stash[chunk] + own_stash[chunk])
        if chunk == 0:
            run(mirror_inflow)
        forward(
            chunk, x_own, x_low, lambda: xs_own[...], lambda: xs_low[...],
            f_own, f_low, fs_own, fs_low,
        )
        cols = pl.ds(chunk * part, part)
        relays += run([
            Copy(f_own.at[:, cols], m_own.at[:, cols], m_own.at[:, cols], (section + 1, place), has_next, has_before),
            Copy(f_low.at[:, cols], m_low.at[:, cols], m_low.at[:, cols], (section + 1, place), next_upper, before_upper),
        ])
        firsts += run(to_tokens(f_own, first_out, chunk, "within"))

    for step in range(half):
        ahead, behind = turn(step)
        relays += run([
            Copy(fs_own, ms_own.at[inner], ms_own.at[behind], (section + 1, base + ahead), has_next, has_before),
            Copy(fs_low, ms_low.at[inner], ms_low.at[behind], (section + 1, base + ahead), next_upper, before_upper),
        ])
    for chunk in range(CHUNKS):
        run(up_fresh[chunk] + own_fresh[chunk])
    run(fresh_factors)

    backs = []
    for chunk in range(CHUNKS):
        if chunk == 0:
            arrive(stash_factors)
        arrive(up_stash[chunk], own_grad[chunk], own_stash[chunk])
        backward(chunk)
        backs += run(to_tokens(dn_low, returned_low, chunk, "down") + to_tokens(dn_own, returned_own, chunk, "within"))

    arrive(relays, fresh_factors, *up_fresh, *own_fresh)
    seconds = []
    for chunk in range(CHUNKS):
        forward(
            chunk, m_own, m_low, lambda: jnp.sum(ms_own[...], axis=0), lambda: jnp.sum(ms_low[...], axis=0),
            s_own, None, None, None,
        )
        seconds += run(to_tokens(s_own, second_out, chunk, "within"))
    arrive(firsts, mirror_inflow, backs, seconds)
    for copy in list(pending):
        copy.sent()


def counts(half):
    remote = CHUNKS * (9 * half + 2) + 9 * half + 16
    return remote, CHUNKS * 8 + 20


def per_device(inflow, fresh, stash_held, grad_in, query_gain, key_gain, value_gain):
    sections, tensors = lax.axis_size("section"), lax.axis_size("tensor")
    half = tensors // 2
    inflow, held, grad = inflow[0], stash_held[0], grad_in[0]
    rows, features = inflow.shape
    length, group = half * rows, features // half
    gains_in = jnp.pad(
        jnp.concatenate([query_gain, key_gain, value_gain], axis=0), ((0, 5), (0, 0))
    )
    tokens = jax.ShapeDtypeStruct((rows, features), bf16)
    any_space = pl.BlockSpec(memory_space=pl.ANY)
    wide = pltpu.VMEM((length, group), bf16)
    narrow = pltpu.VMEM((length, LANES), f32)
    slots = pltpu.VMEM((half, length, LANES), f32)
    remote, local = counts(half)
    first_out, second_out, evicted, stash, returned_own, returned_low = pl.pallas_call(
        functools.partial(kernel, sections, tensors),
        in_specs=[any_space] * 5,
        out_specs=[any_space] * 6,
        out_shape=[tokens] * 6,
        scratch_shapes=[wide] * 12
        + [narrow] * 4
        + [slots] * 2
        + [narrow] * 2
        + [pltpu.VMEM((8, group), f32)]
        + [pltpu.VMEM((rows, features), bf16)] * 3
        + [pltpu.VMEM((rows, LANES), f32)] * 2
        + [pltpu.VMEM((half, rows, LANES), f32)]
        + [
            pltpu.SemaphoreType.DMA((remote,)),
            pltpu.SemaphoreType.DMA((remote,)),
            pltpu.SemaphoreType.DMA((local,)),
        ],
        compiler_params=pltpu.CompilerParams(
            collective_id=0, has_side_effects=True, vmem_limit_bytes=56 * 1024 * 1024
        ),
        cost_estimate=pl.CostEstimate(
            flops=length * length * group * 40,
            bytes_accessed=length * group * 40,
            transcendentals=length * length * group // 16,
        ),
    )(inflow, fresh, held, grad, gains_in)

    received = lax.axis_index("tensor") < half
    returned = returned_own.astype(f32) + jnp.where(received, returned_low.astype(f32), 0.0)
    values = stash.astype(f32)
    factor = lax.rsqrt(jnp.mean(values * values, axis=-1, keepdims=True) + epsilon)
    scaled = values * factor
    inner = factor * jnp.mean(returned * values, axis=-1, keepdims=True)
    grad_out = (grad.astype(f32) + factor * (returned - scaled * inner)).astype(bf16)
    return (first_out[None], second_out[None], evicted[None], grad_out[None])


def solution(mesh):
    tokens = P("section", "tensor", None)
    gain = P("section", "tensor")
    return jax.shard_map(
        per_device,
        mesh=mesh,
        in_specs=(tokens, P("tensor", None), tokens, tokens, gain, gain, gain),
        out_specs=(tokens,) * 4,
        check_vma=False,
    )
```
